32 devices in a mesh: leaf: 16 (over z, y, x), cols: 2 (over core).
Axes of the slice: x: 2, y: 2, z: 4, core: 2. Of those that a mesh axis runs over, the one named last changes fastest.
Arguments:
- vectors: bfloat16 [128, 32768], P('cols', 'leaf'), may hold values from -6 to 6
- near_blocks: bfloat16 [128, 8, 256, 256], P('leaf', None, 'cols'), may hold values from -0.125 to 0.125
- near_index: int32 [128, 8], P('leaf'), may hold values from -1 to 127, as said below
- far_index: int32 [128, 8], P('leaf'), may hold values from -1 to 127, as said below
- far_kind: int32 [128, 8], P('leaf'), may hold values from 0 to 15
- cluster_basis: bfloat16 [128, 64, 256], P('leaf'), may hold values from -0.375 to 0.375
- leaf_transfer: float32 [128, 64, 64], P('leaf'), may hold values from -0.25 to 0.25
- coupling_table: float32 [16, 64, 64], replicated, may hold values from -0.5 to 0.5
- parent_transfer_matrices: float32 [2, 64, 64], replicated, may hold values from -0.625 to 0.625
- coarse_kind: int32 [15], replicated, may hold values from 0 to 15
Outputs:
- product: bfloat16 [128, 32768], P('cols', 'leaf')
The draws below stay inside these ranges and needn't reach their ends.
Inputs may be any that keep to these rules, and one draw needn't show every extreme that they name: `near_index`: row i holds distinct leaves within 8 positions of leaf i, and -1 in unused slots; its first entry is i itself, its second is i - 8 for even i and i + 8 for odd i, or -1 where that is outside the leaves. No leaf stands in both near_index and far_index of one row. `far_index`: row i holds distinct leaves other than i within 8 positions of leaf i, and -1 in unused slots.
All inputs are finite; a program needn't handle non-finite values.
Results may differ from the reference program's by a relative error of at most 0.0044.
Values may be sent and summed in bfloat16 or wider, within the bound.
A program may use at most 128 MiB of HBM per device.

```python
import jax
import jax.numpy as jnp
from jax import lax

LEAF = 256
RANK = 64
COLS = 128
LEAF_DEV = 8
K_NEAR = 8
K_FAR = 8
KINDS = 16
LEAVES = 128
ROWS = 32768
GROUPS = 16
N_LEAF = 16


def window_lists(key):
    key_order = jax.random.fold_in(key, 71)
    key_near = jax.random.fold_in(key, 72)
    key_far = jax.random.fold_in(key, 73)
    candidates = jnp.concatenate([jnp.arange(-LEAF_DEV, 0, dtype=jnp.int32), jnp.arange(1, LEAF_DEV + 1, dtype=jnp.int32)])
    width_count = 2 * LEAF_DEV
    leaf_ids = jnp.arange(LEAVES, dtype=jnp.int32)[:, None]
    forced_offset = jnp.where(leaf_ids % 2 == 0, -LEAF_DEV, LEAF_DEV).astype(jnp.int32)
    is_forced = candidates[None, :] == forced_offset
    scores = jax.random.randint(key_order, (LEAVES, width_count), 0, 1 << 20, dtype=jnp.int32) * width_count + jnp.arange(width_count, dtype=jnp.int32)[None, :]
    scores = jnp.where(is_forced, (1 << 20) * width_count + width_count, scores)
    order = jnp.argsort(scores, axis=1)
    offsets = candidates[order]
    forced_target = leaf_ids + forced_offset
    forced_inside = (forced_target >= 0) & (forced_target < LEAVES)
    forced_entry = jnp.where(forced_inside, forced_target, -1)
    near_live = jax.random.randint(key_near, (LEAVES, 1), 0, K_NEAR - 1, dtype=jnp.int32)
    near_slots = jnp.arange(K_NEAR - 2, dtype=jnp.int32)[None, :] < near_live
    near_targets = leaf_ids + offsets[:, :K_NEAR - 2]
    near_inside = (near_targets >= 0) & (near_targets < LEAVES)
    near_list = jnp.concatenate([leaf_ids, forced_entry, jnp.where(near_slots & near_inside, near_targets, -1)], axis=1)
    far_live = jax.random.randint(key_far, (LEAVES, 1), 1, K_FAR + 1, dtype=jnp.int32)
    far_slots = jnp.arange(K_FAR, dtype=jnp.int32)[None, :] < far_live
    far_targets = leaf_ids + offsets[:, K_NEAR - 2:K_NEAR - 2 + K_FAR]
    far_inside = (far_targets >= 0) & (far_targets < LEAVES)
    far_list = jnp.where(far_slots & far_inside, far_targets, -1)
    return (near_list.astype(jnp.int32), far_list.astype(jnp.int32))


def draw_near_index(key, part):
    return window_lists(key)[0]


def draw_far_index(key, part):
    return window_lists(key)[1]


def touch_ends(drawn, key, smallest, largest):
    dims = drawn.shape
    place = [jax.random.randint(jax.random.fold_in(key, axis), (), 0, dims[axis]) for axis in range(len(dims))]
    drawn = drawn.at[tuple(place)].set(smallest)
    longest = dims.index(max(dims))
    place[longest] = (place[longest] + 1) % dims[longest]
    return drawn.at[tuple(place)].set(largest)


def levels(own_key, shape, pieces, low, high):
    factor_of, own = 1.0, jax.random.fold_in(own_key, 6)
    for axis_at, blocks in pieces:
        draws = jnp.exp(jax.random.uniform(jax.random.fold_in(own, axis_at), (blocks,), jnp.float32, low / len(pieces), high / len(pieces)))
        factor_of = factor_of * jnp.repeat(draws, shape[axis_at] // blocks).reshape([-1 if axis == axis_at else 1 for axis in range(len(shape))])
    return factor_of


def noise(own_key, extent, spread, bound, cuts=(), kind=jnp.bfloat16):
    result = jax.random.normal(own_key, extent, jnp.float32) * spread
    if len(cuts) > 0:
        result = levels(own_key, extent, cuts, -0.22, 0.18) * result
    return jnp.clip(result, min=-bound, max=bound).astype(kind)


def setup_inputs(seed: int = 0) -> dict:
    keys = jax.random.split(jax.random.key(seed), 11)
    vectors = noise(keys[0], (COLS, ROWS), 1.0, 6.0, ((0, 2), (1, 16)))
    near_blocks = noise(keys[1], (LEAVES, K_NEAR, LEAF, LEAF), (LEAF * K_NEAR) ** -0.5, 0.125, ((0, 16), (2, 2)))
    near_index = draw_near_index(jax.random.fold_in(keys[10], 71), 0)
    far_index = draw_far_index(jax.random.fold_in(keys[10], 71), 0)
    far_kind = touch_ends(jax.random.randint(keys[4], (LEAVES, K_FAR), 0, KINDS), jax.random.fold_in(keys[4], 1), 0, KINDS - 1).astype(jnp.int32)
    cluster_basis = noise(keys[5], (LEAVES, RANK, LEAF), LEAF ** -0.5, 0.375, ((0, 16),))
    leaf_transfer = noise(keys[6], (LEAVES, RANK, RANK), (LEAF_DEV * RANK) ** -0.5, 0.25, ((0, 16),), jnp.float32)
    coupling_table = noise(keys[7], (KINDS, RANK, RANK), (2 * RANK) ** -0.5, 0.5, (), jnp.float32)
    parent_transfer_matrices = noise(keys[8], (2, RANK, RANK), (RANK * 7 // 5) ** -0.5, 0.625, (), jnp.float32)
    coarse_kind = touch_ends(jax.random.randint(keys[9], (GROUPS - 1,), 0, KINDS), jax.random.fold_in(keys[9], 1), 0, KINDS - 1).astype(jnp.int32)
    return {"vectors": vectors, "near_blocks": near_blocks, "near_index": near_index, "far_index": far_index, "far_kind": far_kind, "cluster_basis": cluster_basis, "leaf_transfer": leaf_transfer, "coupling_table": coupling_table, "parent_transfer_matrices": parent_transfer_matrices, "coarse_kind": coarse_kind}


def coarse_tree(level_coefs, coarse_kind, coupling_table, parent_transfer_matrices):
    upper_level = lax.Precision.HIGHEST
    depth_count = level_coefs.shape[0].bit_length() - 1
    parent_chain = level_coefs
    couplings = []
    for depth_step in range(depth_count):
        node_count = parent_chain.shape[0]
        left_child_nodes = parent_chain[0::2]
        right_child_nodes = parent_chain[1::2]
        kind_rows = coarse_kind[node_count // 2 - 1:node_count - 1]
        lookup_tables = coupling_table[kind_rows]
        toward_left_child = jnp.einsum('jkw,jvw->jkv', right_child_nodes, lookup_tables, precision=upper_level)
        toward_right_child = jnp.einsum('ufo,uoz->ufz', left_child_nodes, lookup_tables, precision=upper_level)
        couplings.append(jnp.stack([toward_left_child, toward_right_child], axis=1).reshape(parent_chain.shape))
        if depth_step + 1 < depth_count:
            parent_chain = (jnp.einsum('mhw,vw->mhv', left_child_nodes, parent_transfer_matrices[0], precision=upper_level)
                         + jnp.einsum('mhw,vw->mhv', right_child_nodes, parent_transfer_matrices[1], precision=upper_level))
    descending_pass = couplings[-1]
    for depth_step in range(depth_count - 2, -1, -1):
        child_nodes = jnp.stack([jnp.einsum('fno,od->fnd', descending_pass, parent_transfer_matrices[0], precision=upper_level),
                              jnp.einsum('fno,od->fnd', descending_pass, parent_transfer_matrices[1], precision=upper_level)], axis=1)
        descending_pass = child_nodes.reshape(couplings[depth_step].shape) + couplings[depth_step]
    return descending_pass


def reference(vectors, near_blocks, near_index, far_index, far_kind, cluster_basis, leaf_transfer, coupling_table, parent_transfer_matrices, coarse_kind):
    upper_level = lax.Precision.HIGHEST
    leaf_count = cluster_basis.shape[0]
    basis_rank = cluster_basis.shape[1]
    leaf_rows = cluster_basis.shape[2]
    col_count = vectors.shape[0]
    vector_leaves = vectors.astype(jnp.float32).reshape(col_count, leaf_count, leaf_rows)
    basis_wide = cluster_basis.astype(jnp.float32)
    leaf_coefs = jnp.einsum('cir,iqr->icq', vector_leaves, basis_wide, precision=upper_level)
    grouped = leaf_coefs.reshape(N_LEAF, LEAF_DEV, col_count, basis_rank)
    transfers = leaf_transfer.reshape(N_LEAF, LEAF_DEV, basis_rank, basis_rank)
    group_coef = jnp.einsum('gics,girs->gcr', grouped, transfers, precision=upper_level)
    descending_pass = coarse_tree(group_coef, coarse_kind, coupling_table, parent_transfer_matrices)
    repeated = jnp.repeat(descending_pass, LEAF_DEV, axis=0)
    leaf_field = jnp.einsum('icr,irs->ics', repeated, leaf_transfer, precision=upper_level)
    far_sum = jnp.zeros_like(leaf_field)
    for slot_index in range(K_FAR):
        valid = far_index[:, slot_index] >= 0
        target = jnp.where(valid, far_index[:, slot_index], 0).astype(jnp.int32)
        picked = leaf_coefs[target] * valid[:, None, None].astype(jnp.float32)
        chosen = coupling_table[far_kind[:, slot_index]]
        far_sum = far_sum + jnp.einsum('ics,irs->icr', picked, chosen, precision=upper_level)
    leaf_field = leaf_field + far_sum
    field_rounded = lax.optimization_barrier(leaf_field.astype(jnp.bfloat16)).astype(jnp.float32)
    far_rows = jnp.einsum('ics,isq->ciq', field_rounded, basis_wide, precision=upper_level)
    near_sum = jnp.zeros_like(far_rows)
    for slot_index in range(K_NEAR):
        valid = near_index[:, slot_index] >= 0
        target = jnp.where(valid, near_index[:, slot_index], 0).astype(jnp.int32)
        picked_rows = vector_leaves[:, target, :] * valid[None, :, None].astype(jnp.float32)
        blocks = near_blocks[:, slot_index].astype(jnp.float32)
        near_sum = near_sum + jnp.einsum('cir,iqr->ciq', picked_rows, blocks, precision=upper_level)
    return (far_rows + near_sum).reshape(col_count, -1).astype(jnp.bfloat16)
```

```python
import functools

import jax
import jax.numpy as jnp
from jax import lax
from jax.experimental import pallas as pl
from jax.experimental.pallas import tpu as pltpu
from jax.sharding import PartitionSpec as P

HI = lax.Precision.HIGHEST
F32 = jnp.float32
BF16 = jnp.bfloat16
CHUNKS = 2


def nt(a, b, precision=None):
    return lax.dot_general(
        a, b, (((1,), (1,)), ((), ())), precision=precision, preferred_element_type=F32
    )


def nn(a, b, precision=None):
    return jnp.dot(a, b, precision=precision, preferred_element_type=F32)


def kernel(
    n, x_ref, near_hbm, near_idx, far_idx, far_kind, basis, transfer, table, parents, kinds,
    out, xw, cw, blocks, up_out, up_in, near_out, near_in, total, own_near, table16,
    send, recv, local,
):
    me, core = lax.axis_index("leaf"), lax.axis_index("cols")
    other = 1 - core
    leaves, slots = near_idx.shape
    far_slots = far_idx.shape[1]
    rows = basis.shape[2]
    half = near_hbm.shape[2]
    cols = x_ref.shape[0]
    depth = n.bit_length() - 1
    side = lax.rem(me, 2)
    pair = me + 1 - 2 * side
    onward, source = me + 2 - 4 * side, me - 2 + 4 * side
    has_onward = jnp.logical_and(onward >= 0, onward < n)
    has_source = jnp.logical_and(source >= 0, source < n)
    there = side * 2 * leaves
    direct = (1 - side) * 2 * leaves
    relayed = side * 2 * leaves
    part = leaves // CHUNKS
    mirror = lambda l: me + (1 - 2 * (lax.rem(me // (1 << l), 2))) * (1 << l)

    barrier = pltpu.get_barrier_semaphore()

    def greet(leaf, c):
        pl.semaphore_signal(
            barrier, inc=1, device_id=(leaf, c), device_id_type=pl.DeviceIdType.MESH
        )

    greet(me, other)
    greet(pair, core)
    for level in range(2, depth):
        greet(mirror(level), core)

    @pl.when(has_onward)
    def _():
        greet(onward, core)

    @pl.when(has_source)
    def _():
        greet(source, core)

    def fetch(i):
        return pltpu.make_async_copy(near_hbm.at[i], blocks.at[i], local.at[i])

    for i in range(leaves):
        fetch(i).start()
    for i in range(leaves):
        xw[core, leaves + i] = x_ref[:, i * rows : (i + 1) * rows]

    @pl.when(jnp.logical_not(has_source))
    def _():
        xw[0, pl.ds(relayed, leaves)] = jnp.zeros((leaves, cols, rows), BF16)
        xw[1, pl.ds(relayed, leaves)] = jnp.zeros((leaves, cols, rows), BF16)
        cw[pl.ds(relayed, leaves)] = jnp.zeros((leaves,) + cw.shape[1:], BF16)

    peers = depth + has_onward.astype(jnp.int32) + has_source.astype(jnp.int32)
    pl.semaphore_wait(barrier, peers)

    def copy(src, dst, s, leaf, c):
        return pltpu.make_async_remote_copy(
            src_ref=src, dst_ref=dst, send_sem=send.at[s], recv_sem=recv.at[s],
            device_id=(leaf, c), device_id_type=pl.DeviceIdType.MESH,
        )

    def at(c, start, h):
        return xw.at[c, pl.ds(start + h * part, part)]

    def to_pair(h):
        return copy(at(core, leaves, h), at(core, there, h), h, pair, core)

    def from_pair(h):
        return copy(at(core, direct, h), at(core, direct, h), h, pair, core)

    def relay(h):
        return copy(at(core, direct, h), at(core, there, h), CHUNKS + h, onward, core)

    def from_relay(h):
        return copy(at(core, relayed, h), at(core, relayed, h), CHUNKS + h, source, core)

    def across(which, start, h):
        return copy(
            at(core, start, h), at(core, start, h), (2 + which) * CHUNKS + h, me, other
        )

    def from_across(which, start, h):
        return copy(
            at(other, start, h), at(other, start, h), (2 + which) * CHUNKS + h, me, other
        )

    base = 5 * CHUNKS
    own_cw = cw.at[pl.ds(leaves, leaves)]
    direct_cw = cw.at[pl.ds(direct, leaves)]
    relayed_cw = cw.at[pl.ds(relayed, leaves)]
    there_cw = cw.at[pl.ds(there, leaves)]
    coef_pair = copy(own_cw, there_cw, base, pair, core)
    coef_from_pair = copy(direct_cw, direct_cw, base, pair, core)
    coef_relay = copy(direct_cw, there_cw, base + 1, onward, core)
    coef_from_relay = copy(relayed_cw, relayed_cw, base + 1, source, core)

    def up(level):
        return copy(up_out.at[level], up_in.at[level], base + 2 + level, mirror(level), core)

    def near_copy(i):
        return copy(near_out.at[i], near_in.at[i], base + 2 + depth + i, me, other)

    for h in range(CHUNKS):
        to_pair(h).start()
    for h in range(CHUNKS):
        across(0, leaves, h).start()

    ancestor = jnp.zeros((cols, basis.shape[1]), F32)
    for i in range(leaves):
        coef = nt(x_ref[:, i * rows : (i + 1) * rows], basis[i])
        cw[leaves + i] = coef.astype(BF16)
        ancestor += nt(coef, transfer[i], HI)
    up_out[0] = ancestor
    up(0).start()
    coef_pair.start()
    table16[...] = table[...].astype(BF16)

    def hand_on(h):
        from_pair(h).wait_recv()

        @pl.when(has_onward)
        def _():
            relay(h).start()

        across(1, direct, h).start()

    def pass_across(h):
        @pl.when(has_source)
        def _():
            from_relay(h).wait_recv()
            across(2, relayed, h).start()

    def hand_coefs_on():
        coef_from_pair.wait_recv()

        @pl.when(has_onward)
        def _():
            coef_relay.start()

    def coefs_in():
        @pl.when(has_source)
        def _():
            coef_from_relay.wait_recv()

    tasks = [functools.partial(hand_on, h) for h in range(CHUNKS)]
    tasks.insert(1, hand_coefs_on)
    tasks += [functools.partial(pass_across, h) for h in range(CHUNKS)]
    tasks.insert(4, coefs_in)

    couplings = []
    for level in range(depth):
        up(level).wait_recv()
        sibling = up_in[level]
        child = lax.rem(me // (1 << level), 2)
        if level + 1 < depth:
            ancestor = nt(ancestor, parents[child], HI) + nt(sibling, parents[1 - child], HI)
            up_out[level + 1] = ancestor
            up(level + 1).start()
        if tasks:
            tasks.pop(0)()
        number = (n // (2 << level)) + me // (2 << level)
        coupling = table[kinds[number - 1]]
        couplings.append(
            jnp.where(child == 0, nt(sibling, coupling, HI), nn(sibling, coupling, HI))
        )
    down = couplings[depth - 1]
    for level in range(depth - 2, -1, -1):
        child = lax.rem(me // (1 << level), 2)
        down = nn(down, parents[child], HI) + couplings[level]
    for task in tasks:
        task()
    first = (me - 1) * leaves

    def window(index):
        inside = jnp.minimum(jnp.maximum(index - first, 0), 3 * leaves - 1)
        return jnp.where(index >= 0, inside, leaves)

    def far(i, carry):
        field = nn(down, transfer[i], HI)
        for k in range(far_slots):
            index = far_idx[i, k]
            live = index >= 0
            picked = cw[window(index)]
            picked = jnp.where(live, picked, jnp.zeros_like(picked))
            field += nt(picked, table16[far_kind[i, k]])
        total[i] = nn(field.astype(BF16), basis[i])
        return carry

    lax.fori_loop(0, leaves, far, 0)

    for h in range(CHUNKS):
        from_across(0, leaves, h).wait_recv()
        from_across(1, direct, h).wait_recv()

    @pl.when(has_source)
    def _():
        for h in range(CHUNKS):
            from_across(2, relayed, h).wait_recv()

    for i in range(leaves):
        fetch(i).wait()

    def near(i, carry):
        mine = jnp.zeros((cols, half), F32)
        theirs = jnp.zeros((cols, half), F32)
        for k in range(slots):
            index = near_idx[i, k]
            live = index >= 0
            place = window(index)
            picked = jnp.concatenate([xw[core, place], xw[other, place]], axis=0)
            picked = jnp.where(live, picked, jnp.zeros_like(picked))
            both = nt(picked, blocks[i, k])
            mine += both[:cols]
            theirs += both[cols:]
        near_out[i] = theirs
        near_copy(i).start()
        own_near[i] = mine
        return carry

    lax.fori_loop(0, leaves, near, 0)

    here = pl.multiple_of(core * half, half)
    across_half = pl.multiple_of(other * half, half)
    for i in range(leaves):
        out[:, pl.ds(i * rows + here, half)] = (
            total[i, :, pl.ds(here, half)] + own_near[i]
        ).astype(BF16)
    for i in range(leaves):
        near_copy(i).wait_recv()
        out[:, pl.ds(i * rows + across_half, half)] = (
            total[i, :, pl.ds(across_half, half)] + near_in[i]
        ).astype(BF16)

    for h in range(CHUNKS):
        to_pair(h).wait_send()
        across(0, leaves, h).wait_send()
        across(1, direct, h).wait_send()
    coef_pair.wait_send()
    for level in range(depth):
        up(level).wait_send()
    for i in range(leaves):
        near_copy(i).wait_send()

    @pl.when(has_onward)
    def _():
        for h in range(CHUNKS):
            relay(h).wait_send()
        coef_relay.wait_send()

    @pl.when(has_source)
    def _():
        for h in range(CHUNKS):
            across(2, relayed, h).wait_send()


def shards(
    vectors, near_blocks, near_index, far_index, far_kind, cluster_basis, leaf_transfer,
    coupling_table, parent_transfer_matrices, coarse_kind,
):
    n = lax.axis_size("leaf")
    depth = n.bit_length() - 1
    cols = vectors.shape[0]
    leaves, rank, rows = cluster_basis.shape
    half = near_blocks.shape[2]
    copies = 5 * CHUNKS + 2 + depth + leaves
    vmem = pl.BlockSpec(memory_space=pltpu.VMEM)
    smem = pl.BlockSpec(memory_space=pltpu.SMEM)
    hbm = pl.BlockSpec(memory_space=pl.ANY)
    return pl.pallas_call(
        functools.partial(kernel, n),
        out_shape=jax.ShapeDtypeStruct(vectors.shape, BF16),
        in_specs=[vmem, hbm, smem, smem, smem, vmem, vmem, vmem, vmem, smem],
        out_specs=vmem,
        scratch_shapes=[
            pltpu.VMEM((2, 3 * leaves, cols, rows), BF16),
            pltpu.VMEM((3 * leaves, cols, rank), BF16),
            pltpu.VMEM(near_blocks.shape, BF16),
            pltpu.VMEM((depth, cols, rank), F32),
            pltpu.VMEM((depth, cols, rank), F32),
            pltpu.VMEM((leaves, cols, half), F32),
            pltpu.VMEM((leaves, cols, half), F32),
            pltpu.VMEM((leaves, cols, rows), F32),
            pltpu.VMEM((leaves, cols, half), F32),
            pltpu.VMEM(coupling_table.shape, BF16),
            pltpu.SemaphoreType.DMA((copies,)),
            pltpu.SemaphoreType.DMA((copies,)),
            pltpu.SemaphoreType.DMA((leaves,)),
        ],
        compiler_params=pltpu.CompilerParams(
            collective_id=0, has_side_effects=True, vmem_limit_bytes=40 << 20
        ),
        cost_estimate=pl.CostEstimate(flops=10**9, bytes_accessed=6 << 20, transcendentals=0),
    )(
        vectors, near_blocks, near_index, far_index, far_kind, cluster_basis, leaf_transfer,
        coupling_table, parent_transfer_matrices, coarse_kind,
    )


def solution(mesh):
    in_specs = (
        P("cols", "leaf"),
        P("leaf", None, "cols", None),
        P("leaf", None),
        P("leaf", None),
        P("leaf", None),
        P("leaf", None, None),
        P("leaf", None, None),
        P(),
        P(),
        P(),
    )
    out_specs = P("cols", "leaf")
    return jax.shard_map(shards, mesh=mesh, in_specs=in_specs, out_specs=out_specs, check_vma=False)
```

```python
import functools

import jax
import jax.numpy as jnp
from jax import lax
from jax.experimental import pallas as pl
from jax.experimental.pallas import tpu as pltpu
from jax.sharding import PartitionSpec as P

HI = lax.Precision.HIGHEST
F32 = jnp.float32
BF16 = jnp.bfloat16
CHUNKS = 2


def nt(a, b, precision=None):
    return lax.dot_general(
        a, b, (((1,), (1,)), ((), ())), precision=precision, preferred_element_type=F32
    )


def nn(a, b, precision=None):
    return jnp.dot(a, b, precision=precision, preferred_element_type=F32)


def kernel(
    n, x_hbm, near_hbm, near_idx_hbm, far_idx_hbm, far_kind_hbm, basis_hbm, transfer_hbm,
    table_hbm, parents_hbm, kinds_hbm,
    out, xw, cw, blocks, up_out, up_in, near_out, near_in, total, own_near, fields, table16,
    near_idx, far_idx, far_kind, kinds, basis, transfer, table, parents,
    send, recv, local, staged,
):
    me, core = lax.axis_index("leaf"), lax.axis_index("cols")
    other = 1 - core
    leaves, slots = near_idx.shape
    far_slots = far_idx.shape[1]
    rows = basis.shape[2]
    half = near_hbm.shape[2]
    cols = x_hbm.shape[0]
    depth = n.bit_length() - 1
    side = lax.rem(me, 2)
    pair = me + 1 - 2 * side
    onward, source = me + 2 - 4 * side, me - 2 + 4 * side
    has_onward = jnp.logical_and(onward >= 0, onward < n)
    has_source = jnp.logical_and(source >= 0, source < n)
    there = side * 2 * leaves
    direct = (1 - side) * 2 * leaves
    relayed = side * 2 * leaves
    part = leaves // CHUNKS
    mirror = lambda l: me + (1 - 2 * (lax.rem(me // (1 << l), 2))) * (1 << l)

    barrier = pltpu.get_barrier_semaphore()

    def greet(leaf, c):
        pl.semaphore_signal(
            barrier, inc=1, device_id=(leaf, c), device_id_type=pl.DeviceIdType.MESH
        )

    greet(me, other)
    greet(pair, core)
    for level in range(2, depth):
        greet(mirror(level), core)

    @pl.when(has_onward)
    def _():
        greet(onward, core)

    @pl.when(has_source)
    def _():
        greet(source, core)

    def fetch(i):
        return pltpu.make_async_copy(near_hbm.at[i], blocks.at[i], local.at[i])

    def own(i):
        return pltpu.make_async_copy(
            x_hbm.at[:, pl.ds(i * rows, rows)], xw.at[core, leaves + i], staged.at[i]
        )

    inputs = [
        (basis_hbm, basis), (transfer_hbm, transfer), (parents_hbm, parents), (kinds_hbm, kinds),
        (table_hbm, table), (far_idx_hbm, far_idx), (far_kind_hbm, far_kind),
        (near_idx_hbm, near_idx),
    ]
    stages = [
        pltpu.make_async_copy(src, dst, staged.at[leaves + j])
        for j, (src, dst) in enumerate(inputs)
    ]
    for i in range(leaves):
        own(i).start()
    for stage in stages:
        stage.start()
    for i in range(leaves):
        fetch(i).start()
    xw[0, 3 * leaves] = jnp.zeros((cols, rows), BF16)
    xw[1, 3 * leaves] = jnp.zeros((cols, rows), BF16)
    cw[3 * leaves] = jnp.zeros(cw.shape[1:], BF16)

    @pl.when(jnp.logical_not(has_source))
    def _():
        xw[0, pl.ds(relayed, leaves)] = jnp.zeros((leaves, cols, rows), BF16)
        xw[1, pl.ds(relayed, leaves)] = jnp.zeros((leaves, cols, rows), BF16)
        cw[pl.ds(relayed, leaves)] = jnp.zeros((leaves,) + cw.shape[1:], BF16)

    for i in range(leaves):
        own(i).wait()
    peers = depth + has_onward.astype(jnp.int32) + has_source.astype(jnp.int32)
    pl.semaphore_wait(barrier, peers)

    def copy(src, dst, s, leaf, c):
        return pltpu.make_async_remote_copy(
            src_ref=src, dst_ref=dst, send_sem=send.at[s], recv_sem=recv.at[s],
            device_id=(leaf, c), device_id_type=pl.DeviceIdType.MESH,
        )

    def at(c, start, h):
        return xw.at[c, pl.ds(start + h * part, part)]

    def to_pair(h):
        return copy(at(core, leaves, h), at(core, there, h), h, pair, core)

    def from_pair(h):
        return copy(at(core, direct, h), at(core, direct, h), h, pair, core)

    def relay(h):
        return copy(at(core, direct, h), at(core, there, h), CHUNKS + h, onward, core)

    def from_relay(h):
        return copy(at(core, relayed, h), at(core, relayed, h), CHUNKS + h, source, core)

    def across(which, start, h):
        return copy(
            at(core, start, h), at(core, start, h), (2 + which) * CHUNKS + h, me, other
        )

    def from_across(which, start, h):
        return copy(
            at(other, start, h), at(other, start, h), (2 + which) * CHUNKS + h, me, other
        )

    base = 5 * CHUNKS
    own_cw = cw.at[pl.ds(leaves, leaves)]
    direct_cw = cw.at[pl.ds(direct, leaves)]
    relayed_cw = cw.at[pl.ds(relayed, leaves)]
    there_cw = cw.at[pl.ds(there, leaves)]
    coef_pair = copy(own_cw, there_cw, base, pair, core)
    coef_from_pair = copy(direct_cw, direct_cw, base, pair, core)
    coef_relay = copy(direct_cw, there_cw, base + 1, onward, core)
    coef_from_relay = copy(relayed_cw, relayed_cw, base + 1, source, core)

    def up(level):
        return copy(up_out.at[level], up_in.at[level], base + 2 + level, mirror(level), core)

    def near_copy(i):
        return copy(near_out.at[i], near_in.at[i], base + 2 + depth + i, me, other)

    for h in range(CHUNKS):
        to_pair(h).start()
    for h in range(CHUNKS):
        across(0, leaves, h).start()

    for stage in stages:
        stage.wait()
    ancestor = jnp.zeros((cols, basis.shape[1]), F32)
    for i in range(leaves):
        coef = nt(xw[core, leaves + i], basis[i])
        cw[leaves + i] = coef.astype(BF16)
        ancestor += nt(coef, transfer[i], HI)
    up_out[0] = ancestor
    up(0).start()
    coef_pair.start()
    table16[...] = table[...].astype(BF16)

    def hand_on(h):
        from_pair(h).wait_recv()

        @pl.when(has_onward)
        def _():
            relay(h).start()

        across(1, direct, h).start()

    def pass_across(h):
        @pl.when(has_source)
        def _():
            from_relay(h).wait_recv()
            across(2, relayed, h).start()

    def hand_coefs_on():
        coef_from_pair.wait_recv()

        @pl.when(has_onward)
        def _():
            coef_relay.start()

    def coefs_in():
        @pl.when(has_source)
        def _():
            coef_from_relay.wait_recv()

    first = (me - 1) * leaves

    def window(index):
        inside = jnp.minimum(jnp.maximum(index - first, 0), 3 * leaves - 1)
        return jnp.where(index >= 0, inside, 3 * leaves)

    def far(i, carry):
        field = jnp.zeros((cols, basis.shape[1]), F32)
        for k in range(far_slots):
            field += nt(cw[window(far_idx[i, k])], table16[far_kind[i, k]])
        fields[i] = field
        return carry

    def far_part(low, high):
        lax.fori_loop(low, high, far, 0, unroll=2)

    tasks = [[functools.partial(hand_on, h)] for h in range(CHUNKS)]
    tasks[0].append(hand_coefs_on)
    tasks.append([functools.partial(pass_across, 0), coefs_in])
    tasks[2].append(functools.partial(far_part, 0, leaves // 2))
    tasks.append([functools.partial(pass_across, h) for h in range(1, CHUNKS)])
    tasks[3].append(functools.partial(far_part, leaves // 2, leaves))

    couplings = []
    for level in range(depth):
        child = lax.rem(me // (1 << level), 2)
        ours = nt(ancestor, parents[child], HI)
        for task in tasks.pop(0) if tasks else []:
            task()
        up(level).wait_recv()
        sibling = up_in[level]
        if level + 1 < depth:
            ancestor = ours + nt(sibling, parents[1 - child], HI)
            up_out[level + 1] = ancestor
            up(level + 1).start()
        number = (n // (2 << level)) + me // (2 << level)
        coupling = table[kinds[number - 1]]
        couplings.append(
            jnp.where(child == 0, nt(sibling, coupling, HI), nn(sibling, coupling, HI))
        )
    for later in tasks:
        for task in later:
            task()

    for h in range(CHUNKS):
        from_across(0, leaves, h).wait_recv()
        from_across(1, direct, h).wait_recv()

    @pl.when(has_source)
    def _():
        for h in range(CHUNKS):
            from_across(2, relayed, h).wait_recv()

    for i in range(leaves):
        fetch(i).wait()

    def near(i, carry):
        places = [window(near_idx[i, k]) for k in range(slots)]
        block = jnp.concatenate([blocks[i, k] for k in range(slots)], axis=1)
        theirs = jnp.concatenate([xw[other, p] for p in places], axis=1)
        mine = jnp.concatenate([xw[core, p] for p in places], axis=1)
        both = nt(jnp.concatenate([theirs, mine], axis=0), block)
        near_out[i] = both[:cols]
        near_copy(i).start()
        own_near[i] = both[cols:]
        return carry

    lax.fori_loop(0, leaves, near, 0)

    down = couplings[depth - 1]
    for level in range(depth - 2, -1, -1):
        child = lax.rem(me // (1 << level), 2)
        down = nn(down, parents[child], HI) + couplings[level]

    def expand(i, carry):
        field = nn(down, transfer[i], HI) + fields[i]
        total[i] = nn(field.astype(BF16), basis[i])
        return carry

    lax.fori_loop(0, leaves, expand, 0, unroll=2)

    here = pl.multiple_of(core * half, half)
    across_half = pl.multiple_of(other * half, half)
    for i in range(leaves):
        out[:, pl.ds(i * rows + here, half)] = (
            total[i, :, pl.ds(here, half)] + own_near[i]
        ).astype(BF16)
    for i in range(leaves):
        near_copy(i).wait_recv()
        out[:, pl.ds(i * rows + across_half, half)] = (
            total[i, :, pl.ds(across_half, half)] + near_in[i]
        ).astype(BF16)

    for h in range(CHUNKS):
        to_pair(h).wait_send()
        across(0, leaves, h).wait_send()
        across(1, direct, h).wait_send()
    coef_pair.wait_send()
    for level in range(depth):
        up(level).wait_send()
    for i in range(leaves):
        near_copy(i).wait_send()

    @pl.when(has_onward)
    def _():
        for h in range(CHUNKS):
            relay(h).wait_send()
        coef_relay.wait_send()

    @pl.when(has_source)
    def _():
        for h in range(CHUNKS):
            across(2, relayed, h).wait_send()


def shards(
    vectors, near_blocks, near_index, far_index, far_kind, cluster_basis, leaf_transfer,
    coupling_table, parent_transfer_matrices, coarse_kind,
):
    n = lax.axis_size("leaf")
    depth = n.bit_length() - 1
    cols = vectors.shape[0]
    leaves, rank, rows = cluster_basis.shape
    half = near_blocks.shape[2]
    copies = 5 * CHUNKS + 2 + depth + leaves
    vmem = pl.BlockSpec(memory_space=pltpu.VMEM)
    hbm = pl.BlockSpec(memory_space=pltpu.HBM)
    return pl.pallas_call(
        functools.partial(kernel, n),
        out_shape=jax.ShapeDtypeStruct(vectors.shape, BF16),
        in_specs=[hbm] * 10,
        out_specs=vmem,
        scratch_shapes=[
            pltpu.VMEM((2, 3 * leaves + 1, cols, rows), BF16),
            pltpu.VMEM((3 * leaves + 1, cols, rank), BF16),
            pltpu.VMEM(near_blocks.shape, BF16),
            pltpu.VMEM((depth, cols, rank), F32),
            pltpu.VMEM((depth, cols, rank), F32),
            pltpu.VMEM((leaves, cols, half), F32),
            pltpu.VMEM((leaves, cols, half), F32),
            pltpu.VMEM((leaves, cols, rows), F32),
            pltpu.VMEM((leaves, cols, half), F32),
            pltpu.VMEM((leaves, cols, rank), F32),
            pltpu.VMEM(coupling_table.shape, BF16),
            pltpu.SMEM(near_index.shape, jnp.int32),
            pltpu.SMEM(far_index.shape, jnp.int32),
            pltpu.SMEM(far_kind.shape, jnp.int32),
            pltpu.SMEM(coarse_kind.shape, jnp.int32),
            pltpu.VMEM(cluster_basis.shape, BF16),
            pltpu.VMEM(leaf_transfer.shape, F32),
            pltpu.VMEM(coupling_table.shape, F32),
            pltpu.VMEM(parent_transfer_matrices.shape, F32),
            pltpu.SemaphoreType.DMA((copies,)),
            pltpu.SemaphoreType.DMA((copies,)),
            pltpu.SemaphoreType.DMA((leaves,)),
            pltpu.SemaphoreType.DMA((leaves + 8,)),
        ],
        compiler_params=pltpu.CompilerParams(
            collective_id=0, has_side_effects=True, vmem_limit_bytes=60 << 20
        ),
        cost_estimate=pl.CostEstimate(flops=10**9, bytes_accessed=6 << 20, transcendentals=0),
    )(
        vectors, near_blocks, near_index, far_index, far_kind, cluster_basis, leaf_transfer,
        coupling_table, parent_transfer_matrices, coarse_kind,
    )


def solution(mesh):
    in_specs = (
        P("cols", "leaf"),
        P("leaf", None, "cols", None),
        P("leaf", None),
        P("leaf", None),
        P("leaf", None),
        P("leaf", None, None),
        P("leaf", None, None),
        P(),
        P(),
        P(),
    )
    out_specs = P("cols", "leaf")
    return jax.shard_map(shards, mesh=mesh, in_specs=in_specs, out_specs=out_specs, check_vma=False)
```

```python
import functools

import jax
import jax.numpy as jnp
from jax import lax
from jax.experimental import pallas as pl
from jax.experimental.pallas import tpu as pltpu
from jax.sharding import PartitionSpec as P

HI = lax.Precision.HIGHEST
F32 = jnp.float32
BF16 = jnp.bfloat16
CHUNKS = 2


def nt(a, b, precision=None):
    return lax.dot_general(
        a, b, (((1,), (1,)), ((), ())), precision=precision, preferred_element_type=F32
    )


def nn(a, b, precision=None):
    return jnp.dot(a, b, precision=precision, preferred_element_type=F32)


def kernel(
    n, x_hbm, near_hbm, near_idx_hbm, far_idx_hbm, far_kind_hbm, basis_hbm, transfer_hbm,
    table_hbm, parents_hbm, kinds_hbm,
    out, xw, cw, blocks, up_out, up_in, near_out, near_in, total, own_near, fields, table16,
    near_idx, far_idx, far_kind, kinds, basis, transfer, table, parents,
    send, recv, local, staged,
):
    me, core = lax.axis_index("leaf"), lax.axis_index("cols")
    other = 1 - core
    leaves, slots = near_idx.shape
    far_slots = far_idx.shape[1]
    rows = basis.shape[2]
    half = near_hbm.shape[2]
    cols = x_hbm.shape[0]
    depth = n.bit_length() - 1
    side = lax.rem(me, 2)
    pair = me + 1 - 2 * side
    onward, source = me + 2 - 4 * side, me - 2 + 4 * side
    has_onward = jnp.logical_and(onward >= 0, onward < n)
    has_source = jnp.logical_and(source >= 0, source < n)
    there = side * 2 * leaves
    direct = (1 - side) * 2 * leaves
    relayed = side * 2 * leaves
    part = leaves // CHUNKS
    mirror = lambda l: me + (1 - 2 * (lax.rem(me // (1 << l), 2))) * (1 << l)

    barrier = pltpu.get_barrier_semaphore()

    def greet(leaf, c):
        pl.semaphore_signal(
            barrier, inc=1, device_id=(leaf, c), device_id_type=pl.DeviceIdType.MESH
        )

    greet(me, other)
    greet(pair, core)
    for level in range(2, depth):
        greet(mirror(level), core)

    @pl.when(has_onward)
    def _():
        greet(onward, core)

    @pl.when(has_source)
    def _():
        greet(source, core)

    def fetch(i):
        return pltpu.make_async_copy(near_hbm.at[i], blocks.at[i], local.at[i])

    def own(i):
        return pltpu.make_async_copy(
            x_hbm.at[:, pl.ds(i * rows, rows)], xw.at[core, leaves + i], staged.at[i]
        )

    inputs = [
        (basis_hbm, basis), (transfer_hbm, transfer), (parents_hbm, parents), (kinds_hbm, kinds),
        (table_hbm, table), (far_idx_hbm, far_idx), (far_kind_hbm, far_kind),
        (near_idx_hbm, near_idx),
    ]
    stages = [
        pltpu.make_async_copy(src, dst, staged.at[leaves + j])
        for j, (src, dst) in enumerate(inputs)
    ]
    for i in range(leaves):
        own(i).start()
    for stage in stages:
        stage.start()
    for i in range(leaves):
        fetch(i).start()
    xw[0, 3 * leaves] = jnp.zeros((cols, rows), BF16)
    xw[1, 3 * leaves] = jnp.zeros((cols, rows), BF16)
    cw[3 * leaves] = jnp.zeros(cw.shape[1:], BF16)

    @pl.when(jnp.logical_not(has_source))
    def _():
        xw[0, pl.ds(relayed, leaves)] = jnp.zeros((leaves, cols, rows), BF16)
        xw[1, pl.ds(relayed, leaves)] = jnp.zeros((leaves, cols, rows), BF16)
        cw[pl.ds(relayed, leaves)] = jnp.zeros((leaves,) + cw.shape[1:], BF16)

    for i in range(leaves):
        own(i).wait()
    peers = depth + has_onward.astype(jnp.int32) + has_source.astype(jnp.int32)
    pl.semaphore_wait(barrier, peers)

    def copy(src, dst, s, leaf, c):
        return pltpu.make_async_remote_copy(
            src_ref=src, dst_ref=dst, send_sem=send.at[s], recv_sem=recv.at[s],
            device_id=(leaf, c), device_id_type=pl.DeviceIdType.MESH,
        )

    def at(c, start, h):
        return xw.at[c, pl.ds(start + h * part, part)]

    def to_pair(h):
        return copy(at(core, leaves, h), at(core, there, h), h, pair, core)

    def from_pair(h):
        return copy(at(core, direct, h), at(core, direct, h), h, pair, core)

    def relay(h):
        return copy(at(core, direct, h), at(core, there, h), CHUNKS + h, onward, core)

    def from_relay(h):
        return copy(at(core, relayed, h), at(core, relayed, h), CHUNKS + h, source, core)

    def across(which, start, h):
        return copy(
            at(core, start, h), at(core, start, h), (2 + which) * CHUNKS + h, me, other
        )

    def from_across(which, start, h):
        return copy(
            at(other, start, h), at(other, start, h), (2 + which) * CHUNKS + h, me, other
        )

    base = 5 * CHUNKS
    own_cw = cw.at[pl.ds(leaves, leaves)]
    direct_cw = cw.at[pl.ds(direct, leaves)]
    relayed_cw = cw.at[pl.ds(relayed, leaves)]
    there_cw = cw.at[pl.ds(there, leaves)]
    coef_pair = copy(own_cw, there_cw, base, pair, core)
    coef_from_pair = copy(direct_cw, direct_cw, base, pair, core)
    coef_relay = copy(direct_cw, there_cw, base + 1, onward, core)
    coef_from_relay = copy(relayed_cw, relayed_cw, base + 1, source, core)

    def up(level):
        return copy(up_out.at[level], up_in.at[level], base + 2 + level, mirror(level), core)

    def near_copy(i):
        return copy(near_out.at[i], near_in.at[i], base + 2 + depth + i, me, other)

    for stage in stages:
        stage.wait()
    ancestor = jnp.zeros((cols, basis.shape[1]), F32)
    for i in range(leaves):
        coef = nt(xw[core, leaves + i], basis[i])
        cw[leaves + i] = coef.astype(BF16)
        ancestor += nt(coef, transfer[i], HI)
    up_out[0] = ancestor
    up(0).start()
    for h in range(CHUNKS):
        to_pair(h).start()
        if h == 0:
            coef_pair.start()
    for h in range(CHUNKS):
        across(0, leaves, h).start()
    table16[...] = table[...].astype(BF16)

    def hand_on(h):
        from_pair(h).wait_recv()

        @pl.when(has_onward)
        def _():
            relay(h).start()

        across(1, direct, h).start()

    def pass_across(h):
        @pl.when(has_source)
        def _():
            from_relay(h).wait_recv()
            across(2, relayed, h).start()

    def hand_coefs_on():
        coef_from_pair.wait_recv()

        @pl.when(has_onward)
        def _():
            coef_relay.start()

    def coefs_in():
        @pl.when(has_source)
        def _():
            coef_from_relay.wait_recv()

    first = (me - 1) * leaves

    def window(index):
        inside = jnp.minimum(jnp.maximum(index - first, 0), 3 * leaves - 1)
        return jnp.where(index >= 0, inside, 3 * leaves)

    def far(i, carry):
        field = jnp.zeros((cols, basis.shape[1]), F32)
        for k in range(far_slots):
            field += nt(cw[window(far_idx[i, k])], table16[far_kind[i, k]])
        fields[i] = field
        return carry

    def far_part(low, high):
        lax.fori_loop(low, high, far, 0, unroll=2)

    tasks = [[functools.partial(hand_on, h)] for h in range(CHUNKS)]
    tasks[0].append(hand_coefs_on)
    tasks.append([functools.partial(pass_across, 0), coefs_in])
    tasks[2].append(functools.partial(far_part, 0, leaves // 2))
    tasks.append([functools.partial(pass_across, h) for h in range(1, CHUNKS)])
    tasks[3].append(functools.partial(far_part, leaves // 2, leaves))

    couplings = []
    for level in range(depth):
        child = lax.rem(me // (1 << level), 2)
        ours = nt(ancestor, parents[child], HI)
        up(level).wait_recv()
        sibling = up_in[level]
        if level + 1 < depth:
            ancestor = ours + nt(sibling, parents[1 - child], HI)
            up_out[level + 1] = ancestor
            up(level + 1).start()
        for task in tasks.pop(0) if tasks else []:
            task()
        number = (n // (2 << level)) + me // (2 << level)
        coupling = table[kinds[number - 1]]
        couplings.append(
            jnp.where(child == 0, nt(sibling, coupling, HI), nn(sibling, coupling, HI))
        )
    for later in tasks:
        for task in later:
            task()

    for h in range(CHUNKS):
        from_across(0, leaves, h).wait_recv()
        from_across(1, direct, h).wait_recv()

    @pl.when(has_source)
    def _():
        for h in range(CHUNKS):
            from_across(2, relayed, h).wait_recv()

    for i in range(leaves):
        fetch(i).wait()

    def near(i, carry):
        places = [window(near_idx[i, k]) for k in range(slots)]
        block = jnp.concatenate([blocks[i, k] for k in range(slots)], axis=1)
        theirs = jnp.concatenate([xw[other, p] for p in places], axis=1)
        mine = jnp.concatenate([xw[core, p] for p in places], axis=1)
        both = nt(jnp.concatenate([theirs, mine], axis=0), block)
        near_out[i] = both[:cols]
        near_copy(i).start()
        own_near[i] = both[cols:]
        return carry

    lax.fori_loop(0, leaves, near, 0)

    down = couplings[depth - 1]
    for level in range(depth - 2, -1, -1):
        child = lax.rem(me // (1 << level), 2)
        down = nn(down, parents[child], HI) + couplings[level]

    def expand(i, carry):
        field = nn(down, transfer[i], HI) + fields[i]
        total[i] = nn(field.astype(BF16), basis[i])
        return carry

    lax.fori_loop(0, leaves, expand, 0, unroll=2)

    here = pl.multiple_of(core * half, half)
    across_half = pl.multiple_of(other * half, half)
    for i in range(leaves):
        out[:, pl.ds(i * rows + here, half)] = (
            total[i, :, pl.ds(here, half)] + own_near[i]
        ).astype(BF16)
    for i in range(leaves):
        near_copy(i).wait_recv()
        out[:, pl.ds(i * rows + across_half, half)] = (
            total[i, :, pl.ds(across_half, half)] + near_in[i]
        ).astype(BF16)

    for h in range(CHUNKS):
        to_pair(h).wait_send()
        across(0, leaves, h).wait_send()
        across(1, direct, h).wait_send()
    coef_pair.wait_send()
    for level in range(depth):
        up(level).wait_send()
    for i in range(leaves):
        near_copy(i).wait_send()

    @pl.when(has_onward)
    def _():
        for h in range(CHUNKS):
            relay(h).wait_send()
        coef_relay.wait_send()

    @pl.when(has_source)
    def _():
        for h in range(CHUNKS):
            across(2, relayed, h).wait_send()


def shards(
    vectors, near_blocks, near_index, far_index, far_kind, cluster_basis, leaf_transfer,
    coupling_table, parent_transfer_matrices, coarse_kind,
):
    n = lax.axis_size("leaf")
    depth = n.bit_length() - 1
    cols = vectors.shape[0]
    leaves, rank, rows = cluster_basis.shape
    half = near_blocks.shape[2]
    copies = 5 * CHUNKS + 2 + depth + leaves
    vmem = pl.BlockSpec(memory_space=pltpu.VMEM)
    hbm = pl.BlockSpec(memory_space=pltpu.HBM)
    return pl.pallas_call(
        functools.partial(kernel, n),
        out_shape=jax.ShapeDtypeStruct(vectors.shape, BF16),
        in_specs=[hbm] * 10,
        out_specs=vmem,
        scratch_shapes=[
            pltpu.VMEM((2, 3 * leaves + 1, cols, rows), BF16),
            pltpu.VMEM((3 * leaves + 1, cols, rank), BF16),
            pltpu.VMEM(near_blocks.shape, BF16),
            pltpu.VMEM((depth, cols, rank), F32),
            pltpu.VMEM((depth, cols, rank), F32),
            pltpu.VMEM((leaves, cols, half), F32),
            pltpu.VMEM((leaves, cols, half), F32),
            pltpu.VMEM((leaves, cols, rows), F32),
            pltpu.VMEM((leaves, cols, half), F32),
            pltpu.VMEM((leaves, cols, rank), F32),
            pltpu.VMEM(coupling_table.shape, BF16),
            pltpu.SMEM(near_index.shape, jnp.int32),
            pltpu.SMEM(far_index.shape, jnp.int32),
            pltpu.SMEM(far_kind.shape, jnp.int32),
            pltpu.SMEM(coarse_kind.shape, jnp.int32),
            pltpu.VMEM(cluster_basis.shape, BF16),
            pltpu.VMEM(leaf_transfer.shape, F32),
            pltpu.VMEM(coupling_table.shape, F32),
            pltpu.VMEM(parent_transfer_matrices.shape, F32),
            pltpu.SemaphoreType.DMA((copies,)),
            pltpu.SemaphoreType.DMA((copies,)),
            pltpu.SemaphoreType.DMA((leaves,)),
            pltpu.SemaphoreType.DMA((leaves + 8,)),
        ],
        compiler_params=pltpu.CompilerParams(
            collective_id=0, has_side_effects=True, vmem_limit_bytes=60 << 20
        ),
        cost_estimate=pl.CostEstimate(flops=10**9, bytes_accessed=6 << 20, transcendentals=0),
    )(
        vectors, near_blocks, near_index, far_index, far_kind, cluster_basis, leaf_transfer,
        coupling_table, parent_transfer_matrices, coarse_kind,
    )


def solution(mesh):
    in_specs = (
        P("cols", "leaf"),
        P("leaf", None, "cols", None),
        P("leaf", None),
        P("leaf", None),
        P("leaf", None),
        P("leaf", None, None),
        P("leaf", None, None),
        P(),
        P(),
        P(),
    )
    out_specs = P("cols", "leaf")
    return jax.shard_map(shards, mesh=mesh, in_specs=in_specs, out_specs=out_specs, check_vma=False)
```

```python
import functools

import jax
import jax.numpy as jnp
from jax import lax
from jax.experimental import pallas as pl
from jax.experimental.pallas import tpu as pltpu
from jax.sharding import PartitionSpec as P

F32 = jnp.float32
BF16 = jnp.bfloat16
CHUNKS = 2


def split(a):
    high = a.astype(BF16)
    return high, (a - high.astype(F32)).astype(BF16)


def dot(a, b, dims, wide):
    product = functools.partial(
        lax.dot_general, dimension_numbers=(dims, ((), ())), preferred_element_type=F32
    )
    if not wide:
        return product(a, b)
    (a_high, a_low), (b_high, b_low) = split(a), split(b)
    return product(a_high, b_high) + (product(a_high, b_low) + product(a_low, b_high))


def nt(a, b, wide=False):
    return dot(a, b, ((1,), (1,)), wide)


def nn(a, b, wide=False):
    return dot(a, b, ((1,), (0,)), wide)


def kernel(
    n, x_hbm, near_hbm, near_idx_hbm, far_idx_hbm, far_kind_hbm, basis_hbm, transfer_hbm,
    table_hbm, parents_hbm, kinds_hbm,
    out, xw, cw, blocks, up_out, up_in, near_out, near_in, total, own_near, fields, table16,
    near_idx, far_idx, far_kind, kinds, basis, transfer, table, parents,
    send, recv, local, staged,
):
    me, core = lax.axis_index("leaf"), lax.axis_index("cols")
    other = 1 - core
    leaves, slots = near_idx.shape
    far_slots = far_idx.shape[1]
    rows = basis.shape[2]
    half = near_hbm.shape[2]
    cols = x_hbm.shape[0]
    depth = n.bit_length() - 1
    side = lax.rem(me, 2)
    pair = me + 1 - 2 * side
    onward, source = me + 2 - 4 * side, me - 2 + 4 * side
    has_onward = jnp.logical_and(onward >= 0, onward < n)
    has_source = jnp.logical_and(source >= 0, source < n)
    there = side * 2 * leaves
    direct = (1 - side) * 2 * leaves
    relayed = side * 2 * leaves
    part = leaves // CHUNKS
    mirror = lambda l: me + (1 - 2 * (lax.rem(me // (1 << l), 2))) * (1 << l)

    barrier = pltpu.get_barrier_semaphore()

    def greet(leaf, c):
        pl.semaphore_signal(
            barrier, inc=1, device_id=(leaf, c), device_id_type=pl.DeviceIdType.MESH
        )

    greet(me, other)
    greet(pair, core)
    for level in range(2, depth):
        greet(mirror(level), core)

    @pl.when(has_onward)
    def _():
        greet(onward, core)

    @pl.when(has_source)
    def _():
        greet(source, core)

    def fetch(i):
        return pltpu.make_async_copy(near_hbm.at[i], blocks.at[i], local.at[i])

    def own(i):
        return pltpu.make_async_copy(
            x_hbm.at[:, pl.ds(i * rows, rows)], xw.at[core, leaves + i], staged.at[i]
        )

    inputs = [
        (basis_hbm, basis), (transfer_hbm, transfer), (parents_hbm, parents), (kinds_hbm, kinds),
        (table_hbm, table), (far_idx_hbm, far_idx), (far_kind_hbm, far_kind),
        (near_idx_hbm, near_idx),
    ]
    stages = [
        pltpu.make_async_copy(src, dst, staged.at[leaves + j])
        for j, (src, dst) in enumerate(inputs)
    ]
    for i in range(leaves):
        own(i).start()
    for stage in stages:
        stage.start()
    for i in range(leaves):
        fetch(i).start()
    xw[0, 3 * leaves] = jnp.zeros((cols, rows), BF16)
    xw[1, 3 * leaves] = jnp.zeros((cols, rows), BF16)
    cw[3 * leaves] = jnp.zeros(cw.shape[1:], BF16)

    @pl.when(jnp.logical_not(has_source))
    def _():
        xw[0, pl.ds(relayed, leaves)] = jnp.zeros((leaves, cols, rows), BF16)
        xw[1, pl.ds(relayed, leaves)] = jnp.zeros((leaves, cols, rows), BF16)
        cw[pl.ds(relayed, leaves)] = jnp.zeros((leaves,) + cw.shape[1:], BF16)

    for i in range(leaves):
        own(i).wait()
    peers = depth + has_onward.astype(jnp.int32) + has_source.astype(jnp.int32)
    pl.semaphore_wait(barrier, peers)

    def copy(src, dst, s, leaf, c):
        return pltpu.make_async_remote_copy(
            src_ref=src, dst_ref=dst, send_sem=send.at[s], recv_sem=recv.at[s],
            device_id=(leaf, c), device_id_type=pl.DeviceIdType.MESH,
        )

    def at(c, start, h):
        return xw.at[c, pl.ds(start + h * part, part)]

    def to_pair(h):
        return copy(at(core, leaves, h), at(core, there, h), h, pair, core)

    def from_pair(h):
        return copy(at(core, direct, h), at(core, direct, h), h, pair, core)

    def relay(h):
        return copy(at(core, direct, h), at(core, there, h), CHUNKS + h, onward, core)

    def from_relay(h):
        return copy(at(core, relayed, h), at(core, relayed, h), CHUNKS + h, source, core)

    def across(which, start, h):
        return copy(
            at(core, start, h), at(core, start, h), (2 + which) * CHUNKS + h, me, other
        )

    def from_across(which, start, h):
        return copy(
            at(other, start, h), at(other, start, h), (2 + which) * CHUNKS + h, me, other
        )

    base = 5 * CHUNKS
    own_cw = cw.at[pl.ds(leaves, leaves)]
    direct_cw = cw.at[pl.ds(direct, leaves)]
    relayed_cw = cw.at[pl.ds(relayed, leaves)]
    there_cw = cw.at[pl.ds(there, leaves)]
    coef_pair = copy(own_cw, there_cw, base, pair, core)
    coef_from_pair = copy(direct_cw, direct_cw, base, pair, core)
    coef_relay = copy(direct_cw, there_cw, base + 1, onward, core)
    coef_from_relay = copy(relayed_cw, relayed_cw, base + 1, source, core)

    def up(level):
        return copy(up_out.at[level], up_in.at[level], base + 2 + level, mirror(level), core)

    def near_copy(i):
        return copy(near_out.at[i], near_in.at[i], base + 2 + depth + i, me, other)

    for stage in stages:
        stage.wait()
    ancestor = jnp.zeros((cols, basis.shape[1]), F32)
    for i in range(leaves):
        coef = nt(xw[core, leaves + i], basis[i])
        cw[leaves + i] = coef.astype(BF16)
        ancestor += nt(coef, transfer[i], True)
    up_out[0] = ancestor
    up(0).start()
    for h in range(CHUNKS):
        to_pair(h).start()
        if h == 0:
            coef_pair.start()
    for h in range(CHUNKS):
        across(0, leaves, h).start()
    table16[...] = table[...].astype(BF16)

    def hand_on(h):
        from_pair(h).wait_recv()

        @pl.when(has_onward)
        def _():
            relay(h).start()

        across(1, direct, h).start()

    def pass_across(h):
        @pl.when(has_source)
        def _():
            from_relay(h).wait_recv()
            across(2, relayed, h).start()

    def hand_coefs_on():
        coef_from_pair.wait_recv()

        @pl.when(has_onward)
        def _():
            coef_relay.start()

    def coefs_in():
        @pl.when(has_source)
        def _():
            coef_from_relay.wait_recv()

    first = (me - 1) * leaves

    def window(index):
        inside = jnp.minimum(jnp.maximum(index - first, 0), 3 * leaves - 1)
        return jnp.where(index >= 0, inside, 3 * leaves)

    def far(i, carry):
        field = jnp.zeros((cols, basis.shape[1]), F32)
        for k in range(far_slots):
            field += nt(cw[window(far_idx[i, k])], table16[far_kind[i, k]])
        fields[i] = field
        return carry

    def far_part(low, high):
        lax.fori_loop(low, high, far, 0, unroll=2)

    tasks = [[functools.partial(hand_on, h)] for h in range(CHUNKS)]
    tasks[0].append(hand_coefs_on)
    tasks.append([functools.partial(pass_across, 0)])
    tasks.append([functools.partial(pass_across, h) for h in range(1, CHUNKS)])
    tasks[3] += [coefs_in, functools.partial(far_part, 0, leaves)]

    couplings = []
    for level in range(depth):
        child = lax.rem(me // (1 << level), 2)
        ours = nt(ancestor, parents[child], True)
        up(level).wait_recv()
        sibling = up_in[level]
        if level + 1 < depth:
            ancestor = ours + nt(sibling, parents[1 - child], True)
            up_out[level + 1] = ancestor
            up(level + 1).start()
        for task in tasks.pop(0) if tasks else []:
            task()
        number = (n // (2 << level)) + me // (2 << level)
        coupling = table[kinds[number - 1]]
        couplings.append(
            jnp.where(child == 0, nt(sibling, coupling, True), nn(sibling, coupling, True))
        )
    for later in tasks:
        for task in later:
            task()

    for h in range(CHUNKS):
        from_across(0, leaves, h).wait_recv()
        from_across(1, direct, h).wait_recv()

    @pl.when(has_source)
    def _():
        for h in range(CHUNKS):
            from_across(2, relayed, h).wait_recv()

    for i in range(leaves):
        fetch(i).wait()

    def near(i, carry):
        places = [window(near_idx[i, k]) for k in range(slots)]
        block = jnp.concatenate([blocks[i, k] for k in range(slots)], axis=1)
        theirs = jnp.concatenate([xw[other, p] for p in places], axis=1)
        mine = jnp.concatenate([xw[core, p] for p in places], axis=1)
        both = nt(jnp.concatenate([theirs, mine], axis=0), block)
        near_out[i] = both[:cols]
        near_copy(i).start()
        own_near[i] = both[cols:]
        return carry

    lax.fori_loop(0, leaves, near, 0)

    down = couplings[depth - 1]
    for level in range(depth - 2, -1, -1):
        child = lax.rem(me // (1 << level), 2)
        down = nn(down, parents[child], True) + couplings[level]

    def expand(i, carry):
        field = nn(down, transfer[i], True) + fields[i]
        total[i] = nn(field.astype(BF16), basis[i])
        return carry

    lax.fori_loop(0, leaves, expand, 0, unroll=2)

    here = pl.multiple_of(core * half, half)
    across_half = pl.multiple_of(other * half, half)
    for i in range(leaves):
        out[:, pl.ds(i * rows + here, half)] = (
            total[i, :, pl.ds(here, half)] + own_near[i]
        ).astype(BF16)
    for i in range(leaves):
        near_copy(i).wait_recv()
        out[:, pl.ds(i * rows + across_half, half)] = (
            total[i, :, pl.ds(across_half, half)] + near_in[i]
        ).astype(BF16)

    for h in range(CHUNKS):
        to_pair(h).wait_send()
        across(0, leaves, h).wait_send()
        across(1, direct, h).wait_send()
    coef_pair.wait_send()
    for level in range(depth):
        up(level).wait_send()
    for i in range(leaves):
        near_copy(i).wait_send()

    @pl.when(has_onward)
    def _():
        for h in range(CHUNKS):
            relay(h).wait_send()
        coef_relay.wait_send()

    @pl.when(has_source)
    def _():
        for h in range(CHUNKS):
            across(2, relayed, h).wait_send()


def shards(
    vectors, near_blocks, near_index, far_index, far_kind, cluster_basis, leaf_transfer,
    coupling_table, parent_transfer_matrices, coarse_kind,
):
    n = lax.axis_size("leaf")
    depth = n.bit_length() - 1
    cols = vectors.shape[0]
    leaves, rank, rows = cluster_basis.shape
    half = near_blocks.shape[2]
    copies = 5 * CHUNKS + 2 + depth + leaves
    vmem = pl.BlockSpec(memory_space=pltpu.VMEM)
    hbm = pl.BlockSpec(memory_space=pltpu.HBM)
    return pl.pallas_call(
        functools.partial(kernel, n),
        out_shape=jax.ShapeDtypeStruct(vectors.shape, BF16),
        in_specs=[hbm] * 10,
        out_specs=vmem,
        scratch_shapes=[
            pltpu.VMEM((2, 3 * leaves + 1, cols, rows), BF16),
            pltpu.VMEM((3 * leaves + 1, cols, rank), BF16),
            pltpu.VMEM(near_blocks.shape, BF16),
            pltpu.VMEM((depth, cols, rank), F32),
            pltpu.VMEM((depth, cols, rank), F32),
            pltpu.VMEM((leaves, cols, half), F32),
            pltpu.VMEM((leaves, cols, half), F32),
            pltpu.VMEM((leaves, cols, rows), F32),
            pltpu.VMEM((leaves, cols, half), F32),
            pltpu.VMEM((leaves, cols, rank), F32),
            pltpu.VMEM(coupling_table.shape, BF16),
            pltpu.SMEM(near_index.shape, jnp.int32),
            pltpu.SMEM(far_index.shape, jnp.int32),
            pltpu.SMEM(far_kind.shape, jnp.int32),
            pltpu.SMEM(coarse_kind.shape, jnp.int32),
            pltpu.VMEM(cluster_basis.shape, BF16),
            pltpu.VMEM(leaf_transfer.shape, F32),
            pltpu.VMEM(coupling_table.shape, F32),
            pltpu.VMEM(parent_transfer_matrices.shape, F32),
            pltpu.SemaphoreType.DMA((copies,)),
            pltpu.SemaphoreType.DMA((copies,)),
            pltpu.SemaphoreType.DMA((leaves,)),
            pltpu.SemaphoreType.DMA((leaves + 8,)),
        ],
        compiler_params=pltpu.CompilerParams(
            collective_id=0, has_side_effects=True, vmem_limit_bytes=60 << 20
        ),
        cost_estimate=pl.CostEstimate(flops=10**9, bytes_accessed=6 << 20, transcendentals=0),
    )(
        vectors, near_blocks, near_index, far_index, far_kind, cluster_basis, leaf_transfer,
        coupling_table, parent_transfer_matrices, coarse_kind,
    )


def solution(mesh):
    in_specs = (
        P("cols", "leaf"),
        P("leaf", None, "cols", None),
        P("leaf", None),
        P("leaf", None),
        P("leaf", None),
        P("leaf", None, None),
        P("leaf", None, None),
        P(),
        P(),
        P(),
    )
    out_specs = P("cols", "leaf")
    return jax.shard_map(shards, mesh=mesh, in_specs=in_specs, out_specs=out_specs, check_vma=False)
```
